32 devices in a mesh: dom: 1, blk: 4 (over z), grp: 8 (over y, x, core), sub: 1.
Axes of the slice: x: 2, y: 2, z: 4, core: 2. Of those that a mesh axis runs over, the one named last changes fastest.
Arguments:
- records: bfloat16 [512, 8, 1024], P(('dom', 'blk', 'grp')), may hold values from -40 to 40
- flags: int32 [512, 8], P(('dom', 'blk', 'grp')), may hold values 0 or 1
Outputs:
- correlations: bfloat16 [256, 512, 3, 128], P('sub', ('dom', 'blk', 'grp'))
The draws below stay inside these ranges and needn't reach their ends.
All inputs are finite; a program needn't handle non-finite values. No bound on the sum of `flags` on one device may be relied on, other than what follows from the above.
Results may differ from the reference program's by a relative error of at most 0.012.
Values may be sent and summed in bfloat16 or wider, within the bound.
A program may use at most 64 MiB of HBM per device.

```python
import math
import jax
import jax.numpy as jnp
from jax import lax

SEGS = 8
SEG_LEN = 1024
LAGS = 256
STEPS = 3
BINS = 512
BLOCK = 128
CHANNELS = 512
N_BLK = 4
N_SUB = 1


def draw_records(key, part):
    first = jax.random.fold_in(key, 0)
    shape = (CHANNELS, SEGS, SEG_LEN)
    base = jnp.clip(jax.random.normal(first, shape, jnp.float32), -4.0, 4.0)
    colored = base + 0.9 * jnp.roll(base, 1, axis=2) + 0.6 * jnp.roll(base, 2, axis=2)
    return jnp.clip(colored, -40.0, 40.0).astype(jnp.bfloat16)


def plant(entries, rng, smallest, top_value):
    index_at = [jax.random.randint(jax.random.fold_in(rng, axis), (), 0, length) for axis, length in enumerate(entries.shape)]
    main_axis = entries.shape.index(max(entries.shape))
    neighbour = index_at[:main_axis] + [(index_at[main_axis] + 1) % entries.shape[main_axis]] + index_at[main_axis + 1:]
    return entries.at[tuple(index_at)].set(smallest).at[tuple(neighbour)].set(top_value)


def setup_inputs(seed: int = 0, part: int = 0) -> dict:
    keys = jax.random.split(jax.random.key(seed), 3)
    part_splits = jax.random.split(jax.random.fold_in(keys[2], part), 3)
    records = draw_records(jax.random.fold_in(jax.random.fold_in(keys[2], part), 71), part)
    flags = plant((jax.random.randint(part_splits[1], (CHANNELS, SEGS), 0, 4) < 3).astype(jnp.int32), jax.random.fold_in(part_splits[1], 1), 0, 1)
    return {"records": records, "flags": flags}


def lag_tables():
    freq = jnp.arange(BINS, dtype=jnp.int32)
    offset = jnp.arange(LAGS, dtype=jnp.int32) - LAGS // 2
    phase = jnp.mod(freq[:, None] * offset[None, :], SEG_LEN).astype(jnp.float32)
    angle = 2.0 * math.pi * phase / SEG_LEN
    table = jnp.stack([jnp.cos(angle), -jnp.sin(angle)]).astype(jnp.bfloat16)
    return table.astype(jnp.float32)

def reference(records, flags):
    spectra = jnp.fft.rfft(records.astype(jnp.float32), axis=-1)[..., :BINS]
    real_part = jnp.real(spectra).astype(jnp.float32)
    imag_part = jnp.imag(spectra).astype(jnp.float32)
    power = real_part * real_part + imag_part * imag_part
    level = lax.optimization_barrier(jnp.mean(power, axis=-1, keepdims=True))
    valid = flags.astype(jnp.float32)
    scale = valid[..., None] / jnp.sqrt(power + level + 1e-06)
    white = jnp.stack([real_part * scale, imag_part * scale], axis=1).astype(jnp.bfloat16)
    table = lag_tables()
    half = BINS // N_SUB

    def one_block(index):
        first = (index * BLOCK).astype(jnp.int32)
        rows = lax.dynamic_slice_in_dim(white, first, BLOCK, 0).astype(jnp.float32)
        row_flags = lax.dynamic_slice_in_dim(valid, first, BLOCK, 0)
        stacked = jnp.stack([rows.reshape(BLOCK, 2 * SEGS, BINS), jnp.concatenate([rows[:, 1], -rows[:, 0]], axis=1)])
        results = []
        for step in range(STEPS):
            start = (jnp.mod(index - step, N_BLK) * BLOCK).astype(jnp.int32)
            other = lax.dynamic_slice_in_dim(white, start, BLOCK, 0).astype(jnp.float32)
            other = other.reshape(BLOCK, 2 * SEGS, BINS)
            other_flags = lax.dynamic_slice_in_dim(valid, start, BLOCK, 0)
            cross = jnp.einsum('cisf,jsf->cijf', stacked, other, precision=lax.Precision.HIGHEST)
            cross = lax.optimization_barrier(cross.astype(jnp.bfloat16)).astype(jnp.float32)
            total = jnp.zeros((LAGS, BLOCK, BLOCK), jnp.float32)
            for part in range(N_SUB):
                term = jnp.einsum('cfl,cijf->lij', table[:, part * half:(part + 1) * half], cross[..., part * half:(part + 1) * half], precision=lax.Precision.HIGHEST)
                term = lax.optimization_barrier(term.astype(jnp.bfloat16))
                total = total + term.astype(jnp.float32)
            count = jnp.dot(row_flags, other_flags.T, precision=lax.Precision.HIGHEST)
            norm = jnp.sqrt(BINS * jnp.maximum(count, 1.0))
            results.append((total / norm[None]).astype(jnp.bfloat16))
        return jnp.stack(results)
    blocks = lax.map(one_block, jnp.arange(N_BLK, dtype=jnp.int32))
    return blocks.transpose(2, 0, 3, 1, 4).reshape(LAGS, CHANNELS, STEPS, BLOCK)
```

```python
import functools

import jax
import jax.numpy as jnp
import ml_dtypes
import numpy as np
from jax import lax
from jax.experimental import pallas as pl
from jax.experimental.pallas import tpu as pltpu
from jax.sharding import PartitionSpec as P

LAGS = 256
STEPS = 3
LANES = 128
GROUP = 16
MESH = pl.DeviceIdType.MESH


def dft_tables(length):
    bins = length // 2
    phase = np.mod(np.arange(length)[:, None] * np.arange(bins)[None, :], length)
    angle = 2.0 * np.pi * phase / length
    return np.cos(angle).astype(np.float32), (-np.sin(angle)).astype(np.float32)


def lag_tables(length):
    bins = length // 2
    phase = np.mod((np.arange(LAGS) - LAGS // 2)[:, None] * np.arange(bins)[None, :], length)
    angle = 2.0 * np.pi * phase / length
    both = np.stack([np.cos(angle), -np.sin(angle)], axis=1).astype(np.float32)
    return both.astype(ml_dtypes.bfloat16)


def regroup_table(segs):
    per = LANES // GROUP
    table = np.zeros((segs, per, GROUP, per, segs, GROUP), np.float32)
    for s in range(segs):
        for q in range(per):
            for f in range(GROUP):
                table[s, q, f, q, s, f] = 1.0
    size = segs * LANES
    return table.reshape(size, size).astype(ml_dtypes.bfloat16)


def row_table(channels, segs):
    table = np.zeros((segs, channels, channels, segs), np.float32)
    for s in range(segs):
        for c in range(channels):
            table[s, c, c, s] = 1.0
    size = segs * channels
    return table.reshape(size, size).astype(ml_dtypes.bfloat16)


def mm(a, b):
    return jnp.dot(a, b, preferred_element_type=jnp.float32)


def mm_t(a, b):
    return lax.dot_general(a, b, (((1,), (1,)), ((), ())), preferred_element_type=jnp.float32)


def kernel(
    blks, grps, dims, normalise,
    rec_ref, flag_ref, hi_ref, lo_ref, perm_ref, row_ref, lag_ref,
    out_ref, count_ref,
    buf, diag, cross, inv, recv_sem, hop_sem, peer_sem, sib_sem,
):
    channels, segs, bins, half = dims
    width = half * 2 * segs
    chunks = half // GROUP
    pair = channels // 2
    b = lax.axis_index("blk")
    g = lax.axis_index("grp")
    sib = g + 1 - 2 * lax.rem(g, 2)
    peers = [lax.rem(g + 2 * d, grps) for d in range(1, grps // 2)]

    barrier = pltpu.get_barrier_semaphore()
    for k in range(1, STEPS):
        pl.semaphore_signal(barrier, inc=1, device_id={"blk": lax.rem(b + blks - k, blks)}, device_id_type=MESH)
    for other in peers + [sib]:
        pl.semaphore_signal(barrier, inc=1, device_id={"grp": other}, device_id_type=MESH)

    rec = mm(row_ref[...], rec_ref[...]).astype(jnp.bfloat16)
    spec = mm(rec, hi_ref[...]) + mm(rec, lo_ref[...])
    real = spec[:, :bins]
    imag = spec[:, bins:]
    power = real * real + imag * imag
    level = jnp.sum(power, axis=1, keepdims=True) / bins
    scale = 1.0 / jnp.sqrt(power[:, :half] + level + 1e-06)
    flags = flag_ref[...]
    pieces = [(real[:, :half] * scale).astype(jnp.bfloat16), (imag[:, :half] * scale).astype(jnp.bfloat16)]
    rows = []
    for t in range(half // LANES):
        for piece in pieces:
            rows.append(jnp.concatenate([
                piece[s * channels:(s + 1) * channels, t * LANES:(t + 1) * LANES]
                * flags[:, s:s + 1].astype(jnp.bfloat16)
                for s in range(segs)
            ], axis=1))
    regrouped = mm(jnp.concatenate(rows, axis=0), perm_ref[...]).astype(jnp.bfloat16)
    per = LANES // GROUP
    for t in range(half // LANES):
        for i in range(2):
            part = regrouped[(t * 2 + i) * channels:(t * 2 + i + 1) * channels]
            for q in range(per):
                at = ((t * per + q) * 2 + i) * LANES
                buf[0, g, :, at:at + LANES] = part[:, q * LANES:(q + 1) * LANES]
    buf[0, g, :, width:width + LANES] = flags.astype(jnp.bfloat16)

    pl.semaphore_wait(barrier, STEPS - 1 + len(peers) + 1)

    sent = []

    def send(source, k, slot, sem, where):
        copy = pltpu.make_async_remote_copy(
            src_ref=source, dst_ref=buf.at[k, slot], send_sem=sem,
            recv_sem=recv_sem.at[k, slot], device_id=where, device_id_type=MESH,
        )
        copy.start()
        sent.append(copy)

    def arrived(k, slot):
        pltpu.make_async_copy(buf.at[k, slot], buf.at[k, slot], recv_sem.at[k, slot]).wait()

    def spread(k):
        for d, other in enumerate(peers):
            send(buf.at[k, g], k, g, peer_sem.at[k, d], {"grp": other})
        send(buf.at[k, g], k, g, sib_sem.at[k, 0], {"grp": sib})

    def forward(k):
        for d in range(len(peers)):
            slot = lax.rem(g + grps - 2 * (d + 1), grps)
            arrived(k, slot)
            send(buf.at[k, slot], k, slot, sib_sem.at[k, d + 1], {"grp": sib})

    def gather(k):
        for d in range(grps // 2):
            arrived(k, lax.rem(sib + 2 * d, grps))

    for k in range(1, STEPS):
        send(buf.at[0, g], k, g, hop_sem.at[k], {"blk": lax.rem(b + k, blks)})
    spread(0)

    size = 2 * segs * GROUP
    same = (lax.broadcasted_iota(jnp.int32, (channels * GROUP, size), 0) % GROUP
            == lax.broadcasted_iota(jnp.int32, (channels * GROUP, size), 1) % GROUP)

    def build(q, carry):
        at = pl.multiple_of(q * size, size)
        first = buf[0, g, :, pl.ds(at, size)].astype(jnp.float32)
        second = jnp.concatenate([first[:, LANES:], -first[:, :LANES]], axis=1)
        for i, value in enumerate((first, second)):
            wide = jnp.broadcast_to(value[:, None, :], (channels, GROUP, size)).reshape(channels * GROUP, size)
            diag[q, i * channels * GROUP:(i + 1) * channels * GROUP, :] = jnp.where(same, wide, 0.0).astype(jnp.bfloat16)
        return carry

    lax.fori_loop(0, chunks // 2, build, 0)
    arrived(1, g)
    spread(1)
    forward(0)
    lax.fori_loop(chunks // 2, chunks, build, 0)
    arrived(2, g)
    spread(2)
    gather(0)

    block = grps * channels
    for k in range(STEPS):
        tile = buf[k, :, :, width:width + LANES].reshape(block, LANES)
        count = mm_t(flags.astype(jnp.bfloat16), tile)
        count_ref[:, k * block:(k + 1) * block] = count
        factor = lax.rsqrt(bins * jnp.maximum(count, 1.0))
        inv[:, :block] = factor[:pair]
        inv[:, block:] = factor[pair:]

        def multiply(q, carry, k=k):
            at = pl.multiple_of(q * size, size)
            other = buf[k, :, :, pl.ds(at, size)].reshape(block, size)
            product = mm_t(diag[q], other).astype(jnp.bfloat16).reshape(2, 2, pair, GROUP, block)
            low = pl.multiple_of(q * GROUP, GROUP)
            for i in range(2):
                for p in range(2):
                    cross[:, i, pl.ds(low, GROUP), p * block:(p + 1) * block] = product[i, p]
            return carry

        lax.fori_loop(0, chunks, multiply, 0)
        if k + 1 < STEPS:
            forward(k + 1)

        def lag(c, carry, k=k):
            total = mm(lag_ref[...], cross[c].reshape(2 * half, 2 * block)).astype(jnp.bfloat16)
            if normalise:
                total = (total.astype(jnp.float32) * inv[pl.ds(c, 1), :]).astype(jnp.bfloat16)
            out_ref[c, :, k * block:(k + 1) * block] = total[:, :block]
            out_ref[c + pair, :, k * block:(k + 1) * block] = total[:, block:]
            return carry

        lax.fori_loop(0, pair, lag, 0)
        if k + 1 < STEPS:
            gather(k + 1)

    for copy in sent:
        copy.wait_send()


def on_device(records, flags):
    channels, segs, length = records.shape
    bins = length // 2
    splits = lax.axis_size("sub")
    blks = lax.axis_size("blk")
    grps = lax.axis_size("grp")
    half = bins // splits
    block = grps * channels
    cos, sin = dft_tables(length)
    lags = lag_tables(length)
    both = np.stack([cos, sin], axis=1)
    high = both.astype(ml_dtypes.bfloat16)
    low = (both - high.astype(np.float32)).astype(ml_dtypes.bfloat16)
    high, low, lags = jnp.asarray(high), jnp.asarray(low), jnp.asarray(lags)
    if splits > 1:
        first = lax.axis_index("sub") * half
        high = jnp.roll(high, -first, axis=2)
        low = jnp.roll(low, -first, axis=2)
        lags = lax.dynamic_slice_in_dim(lags, first, half, 2)
    width = half * 2 * segs + LANES
    wide_flags = jnp.pad(flags.astype(jnp.float32), ((0, 0), (0, LANES - segs)))
    vmem = pl.BlockSpec(memory_space=pltpu.VMEM)
    out, count = pl.pallas_call(
        functools.partial(kernel, blks, grps, (channels, segs, bins, half), splits == 1),
        out_shape=(
            jax.ShapeDtypeStruct((channels, LAGS, STEPS * block), jnp.bfloat16),
            jax.ShapeDtypeStruct((channels, STEPS * block), jnp.float32),
        ),
        in_specs=[vmem] * 7,
        out_specs=(vmem, vmem),
        scratch_shapes=[
            pltpu.VMEM((STEPS, grps, channels, width), jnp.bfloat16),
            pltpu.VMEM((half // GROUP, 2 * channels * GROUP, 2 * segs * GROUP), jnp.bfloat16),
            pltpu.VMEM((channels // 2, 2, half, 2 * block), jnp.bfloat16),
            pltpu.VMEM((channels // 2, 2 * block), jnp.float32),
            pltpu.SemaphoreType.DMA((STEPS, grps)),
            pltpu.SemaphoreType.DMA((STEPS,)),
            pltpu.SemaphoreType.DMA((STEPS, max(grps // 2 - 1, 1))),
            pltpu.SemaphoreType.DMA((STEPS, grps // 2)),
        ],
        compiler_params=pltpu.CompilerParams(
            collective_id=0, has_side_effects=True, vmem_limit_bytes=48 * 1024 * 1024
        ),
    )(
        records.reshape(channels * segs, length),
        wide_flags,
        high.reshape(length, 2 * bins),
        low.reshape(length, 2 * bins),
        jnp.asarray(regroup_table(segs)),
        jnp.asarray(row_table(channels, segs)),
        lags.reshape(LAGS, 2 * half),
    )
    out = out.transpose(1, 0, 2)
    if splits > 1:
        out = lax.psum_scatter(out, "sub", scatter_dimension=0, tiled=True).astype(jnp.float32)
        out = (out / jnp.sqrt(bins * jnp.maximum(count, 1.0))[None]).astype(jnp.bfloat16)
    return out.reshape(-1, channels, STEPS, block)


def solution(mesh):
    return jax.shard_map(
        on_device,
        mesh=mesh,
        in_specs=(P(("dom", "blk", "grp"), None, None), P(("dom", "blk", "grp"), None)),
        out_specs=P("sub", ("dom", "blk", "grp"), None, None),
        check_vma=False,
    )
```

```python
import functools

import jax
import jax.numpy as jnp
import ml_dtypes
import numpy as np
from jax import lax
from jax.experimental import pallas as pl
from jax.experimental.pallas import tpu as pltpu
from jax.sharding import PartitionSpec as P

LAGS = 256
STEPS = 3
LANES = 128
GROUP = 16
MESH = pl.DeviceIdType.MESH


def dft_tables(length):
    bins = length // 2
    phase = np.mod(np.arange(length)[:, None] * np.arange(bins)[None, :], length)
    angle = 2.0 * np.pi * phase / length
    return np.cos(angle).astype(np.float32), (-np.sin(angle)).astype(np.float32)


def lag_tables(length):
    bins = length // 2
    phase = np.mod((np.arange(LAGS) - LAGS // 2)[:, None] * np.arange(bins)[None, :], length)
    angle = 2.0 * np.pi * phase / length
    both = np.stack([np.cos(angle), -np.sin(angle)], axis=1).astype(np.float32)
    return both.astype(ml_dtypes.bfloat16)


def regroup_table(segs):
    per = LANES // GROUP
    table = np.zeros((segs, per, GROUP, per, segs, GROUP), np.float32)
    for s in range(segs):
        for q in range(per):
            for f in range(GROUP):
                table[s, q, f, q, s, f] = 1.0
    size = segs * LANES
    return table.reshape(size, size).astype(ml_dtypes.bfloat16)


def row_table(channels, segs):
    table = np.zeros((segs, channels, channels, segs), np.float32)
    for s in range(segs):
        for c in range(channels):
            table[s, c, c, s] = 1.0
    size = segs * channels
    return table.reshape(size, size).astype(ml_dtypes.bfloat16)


def mm(a, b):
    return jnp.dot(a, b, preferred_element_type=jnp.float32)


def mm_t(a, b):
    return lax.dot_general(a, b, (((1,), (1,)), ((), ())), preferred_element_type=jnp.float32)


def kernel(
    blks, grps, dims, normalise,
    rec_ref, flag_ref, row_ref, hi_hbm, lo_hbm, perm_hbm, lag_hbm,
    out_ref, count_ref,
    hi_ref, lo_ref, perm_ref, lag_ref, load_sem, buf, diag, cross, inv, recv_sem, hop_sem, peer_sem,
):
    channels, segs, bins, half = dims
    width = half * 2 * segs
    chunks = half // GROUP
    pair = channels // 2
    loads = [
        pltpu.make_async_copy(source, target, load_sem.at[n])
        for n, (source, target) in enumerate(
            ((hi_hbm, hi_ref), (lo_hbm, lo_ref), (perm_hbm, perm_ref), (lag_hbm, lag_ref)))
    ]
    for load in loads:
        load.start()
    b = lax.axis_index("blk")
    g = lax.axis_index("grp")
    sib = g + 1 - 2 * lax.rem(g, 2)
    chip = g // 2
    across = g + 2 - 4 * lax.rem(chip, 2)
    along = g + 4 - 8 * (chip // 2)
    corner = across + 4 - 8 * (chip // 2)
    peers = [across, along]

    barrier = pltpu.get_barrier_semaphore()
    for k in range(1, STEPS):
        pl.semaphore_signal(barrier, inc=1, device_id={"blk": lax.rem(b + blks - k, blks)}, device_id_type=MESH)
    for other in peers + [sib]:
        pl.semaphore_signal(barrier, inc=1, device_id={"grp": other}, device_id_type=MESH)

    rec = mm(row_ref[...], rec_ref[...]).astype(jnp.bfloat16)
    loads[0].wait()
    spec = mm(rec, hi_ref[...])
    loads[1].wait()
    spec = spec + mm(rec, lo_ref[...])
    real = spec[:, :bins]
    imag = spec[:, bins:]
    power = real * real + imag * imag
    level = jnp.sum(power, axis=1, keepdims=True) / bins
    scale = 1.0 / jnp.sqrt(power[:, :half] + level + 1e-06)
    flags = flag_ref[...]
    pieces = [(real[:, :half] * scale).astype(jnp.bfloat16), (imag[:, :half] * scale).astype(jnp.bfloat16)]
    rows = []
    for t in range(half // LANES):
        for piece in pieces:
            rows.append(jnp.concatenate([
                piece[s * channels:(s + 1) * channels, t * LANES:(t + 1) * LANES]
                * flags[:, s:s + 1].astype(jnp.bfloat16)
                for s in range(segs)
            ], axis=1))
    loads[2].wait()
    regrouped = mm(jnp.concatenate(rows, axis=0), perm_ref[...]).astype(jnp.bfloat16)
    per = LANES // GROUP
    for t in range(half // LANES):
        for i in range(2):
            part = regrouped[(t * 2 + i) * channels:(t * 2 + i + 1) * channels]
            for q in range(per):
                at = ((t * per + q) * 2 + i) * LANES
                buf[0, g, :, at:at + LANES] = part[:, q * LANES:(q + 1) * LANES]
    buf[0, g, :, width:width + LANES] = flags.astype(jnp.bfloat16)

    pl.semaphore_wait(barrier, STEPS - 1 + len(peers) + 1)

    sent = []

    cut = width // 2
    rest = width + LANES - cut

    def send(source, target, sems, where):
        copy = pltpu.make_async_remote_copy(
            src_ref=source, dst_ref=target, send_sem=sems[0], recv_sem=sems[1],
            device_id=where, device_id_type=MESH,
        )
        copy.start()
        sent.append(copy)

    def arrived(ref, sem):
        pltpu.make_async_copy(ref, ref, sem).wait()

    def whole(k, slot):
        return buf.at[k, slot]

    def lower(k, slot):
        return buf.at[k, slot, :, pl.ds(0, cut)]

    def upper(k, slot):
        return buf.at[k, slot, :, pl.ds(cut, rest)]

    def to(kind, k):
        return peer_sem.at[k, kind], recv_sem.at[k, kind]

    def hand(k, kind, slot):
        send(whole(k, slot), whole(k, slot), to(kind, k), {"grp": sib})

    def spread(k):
        send(whole(k, g), whole(k, g), to(0, k), {"grp": across})
        send(whole(k, g), whole(k, g), to(1, k), {"grp": along})
        hand(k, 4, g)

    def relay(k):
        arrived(whole(k, across), recv_sem.at[k, 0])
        send(lower(k, across), lower(k, across), to(2, k), {"grp": along})
        hand(k, 5, across)
        arrived(whole(k, along), recv_sem.at[k, 1])
        send(upper(k, along), upper(k, along), to(3, k), {"grp": across})
        hand(k, 6, along)

    def forward(k):
        arrived(lower(k, corner), recv_sem.at[k, 2])
        arrived(upper(k, corner), recv_sem.at[k, 3])
        hand(k, 7, corner)

    def gather(k):
        turn = sib - g
        for kind, slot in ((4, g), (5, across), (6, along), (7, corner)):
            arrived(whole(k, slot + turn), recv_sem.at[k, kind])

    def hopped(k):
        arrived(whole(k, g), hop_sem.at[1, k])

    for k in range(1, STEPS):
        send(whole(0, g), whole(k, g), (hop_sem.at[0, k], hop_sem.at[1, k]), {"blk": lax.rem(b + k, blks)})
    spread(0)

    size = 2 * segs * GROUP
    same = (lax.broadcasted_iota(jnp.int32, (channels * GROUP, size), 0) % GROUP
            == lax.broadcasted_iota(jnp.int32, (channels * GROUP, size), 1) % GROUP)

    def build(q, carry):
        at = pl.multiple_of(q * size, size)
        first = buf[0, g, :, pl.ds(at, size)].astype(jnp.float32)
        second = jnp.concatenate([first[:, LANES:], -first[:, :LANES]], axis=1)
        for i, value in enumerate((first, second)):
            wide = jnp.broadcast_to(value[:, None, :], (channels, GROUP, size)).reshape(channels * GROUP, size)
            diag[q, i * channels * GROUP:(i + 1) * channels * GROUP, :] = jnp.where(same, wide, 0.0).astype(jnp.bfloat16)
        return carry

    lax.fori_loop(0, chunks // 2, build, 0)
    relay(0)
    hopped(1)
    spread(1)
    lax.fori_loop(chunks // 2, chunks, build, 0)
    forward(0)
    hopped(2)
    spread(2)
    relay(1)
    gather(0)

    loads[3].wait()
    block = grps * channels
    for k in range(STEPS):
        tile = buf[k, :, :, width:width + LANES].reshape(block, LANES)
        count = mm_t(flags.astype(jnp.bfloat16), tile)
        count_ref[:, k * block:(k + 1) * block] = count
        factor = lax.rsqrt(bins * jnp.maximum(count, 1.0))
        inv[:, :block] = factor[:pair]
        inv[:, block:] = factor[pair:]

        def multiply(q, carry, k=k):
            at = pl.multiple_of(q * size, size)
            other = buf[k, :, :, pl.ds(at, size)].reshape(block, size)
            product = mm_t(diag[q], other).astype(jnp.bfloat16).reshape(2, 2, pair, GROUP, block)
            low = pl.multiple_of(q * GROUP, GROUP)
            for i in range(2):
                for p in range(2):
                    cross[:, i, pl.ds(low, GROUP), p * block:(p + 1) * block] = product[i, p]
            return carry

        lax.fori_loop(0, chunks, multiply, 0)
        if k + 1 < STEPS:
            if k > 0:
                relay(k + 1)
            forward(k + 1)

        def lag(c, carry, k=k):
            total = mm(lag_ref[...], cross[c].reshape(2 * half, 2 * block)).astype(jnp.bfloat16)
            if normalise:
                total = (total.astype(jnp.float32) * inv[pl.ds(c, 1), :]).astype(jnp.bfloat16)
            out_ref[k, c] = total[:, :block]
            out_ref[k, c + pair] = total[:, block:]
            return carry

        lax.fori_loop(0, pair, lag, 0)
        if k + 1 < STEPS:
            gather(k + 1)

    for copy in sent:
        copy.wait_send()


def on_device(records, flags):
    channels, segs, length = records.shape
    bins = length // 2
    splits = lax.axis_size("sub")
    blks = lax.axis_size("blk")
    grps = lax.axis_size("grp")
    half = bins // splits
    block = grps * channels
    cos, sin = dft_tables(length)
    lags = lag_tables(length)
    both = np.stack([cos, sin], axis=1)
    high = both.astype(ml_dtypes.bfloat16)
    low = (both - high.astype(np.float32)).astype(ml_dtypes.bfloat16)
    high, low, lags = jnp.asarray(high), jnp.asarray(low), jnp.asarray(lags)
    if splits > 1:
        first = lax.axis_index("sub") * half
        high = jnp.roll(high, -first, axis=2)
        low = jnp.roll(low, -first, axis=2)
        lags = lax.dynamic_slice_in_dim(lags, first, half, 2)
    width = half * 2 * segs + LANES
    wide_flags = jnp.pad(flags.astype(jnp.float32), ((0, 0), (0, LANES - segs)))
    vmem = pl.BlockSpec(memory_space=pltpu.VMEM)
    out, count = pl.pallas_call(
        functools.partial(kernel, blks, grps, (channels, segs, bins, half), splits == 1),
        out_shape=(
            jax.ShapeDtypeStruct((STEPS, channels, LAGS, block), jnp.bfloat16),
            jax.ShapeDtypeStruct((channels, STEPS * block), jnp.float32),
        ),
        in_specs=[vmem] * 3 + [pl.BlockSpec(memory_space=pltpu.HBM)] * 4,
        out_specs=(vmem, vmem),
        scratch_shapes=[
            pltpu.VMEM((length, 2 * bins), jnp.bfloat16),
            pltpu.VMEM((length, 2 * bins), jnp.bfloat16),
            pltpu.VMEM((segs * LANES, segs * LANES), jnp.bfloat16),
            pltpu.VMEM((LAGS, 2 * half), jnp.bfloat16),
            pltpu.SemaphoreType.DMA((4,)),
            pltpu.VMEM((STEPS, grps, channels, width), jnp.bfloat16),
            pltpu.VMEM((half // GROUP, 2 * channels * GROUP, 2 * segs * GROUP), jnp.bfloat16),
            pltpu.VMEM((channels // 2, 2, half, 2 * block), jnp.bfloat16),
            pltpu.VMEM((channels // 2, 2 * block), jnp.float32),
            pltpu.SemaphoreType.DMA((STEPS, 8)),
            pltpu.SemaphoreType.DMA((2, STEPS)),
            pltpu.SemaphoreType.DMA((STEPS, 8)),
        ],
        compiler_params=pltpu.CompilerParams(
            collective_id=0, has_side_effects=True, vmem_limit_bytes=62 * 1024 * 1024
        ),
    )(
        records.reshape(channels * segs, length),
        wide_flags,
        jnp.asarray(row_table(channels, segs)),
        high.reshape(length, 2 * bins),
        low.reshape(length, 2 * bins),
        jnp.asarray(regroup_table(segs)),
        lags.reshape(LAGS, 2 * half),
    )
    out = out.transpose(2, 1, 0, 3)
    if splits > 1:
        out = lax.psum_scatter(out, "sub", scatter_dimension=0, tiled=True).astype(jnp.float32)
        out = (out / jnp.sqrt(bins * jnp.maximum(count, 1.0)).reshape(1, channels, STEPS, block)).astype(jnp.bfloat16)
    return out


def solution(mesh):
    return jax.shard_map(
        on_device,
        mesh=mesh,
        in_specs=(P(("dom", "blk", "grp"), None, None), P(("dom", "blk", "grp"), None)),
        out_specs=P("sub", ("dom", "blk", "grp"), None, None),
        check_vma=False,
    )
```

```python
import functools

import jax
import jax.numpy as jnp
import ml_dtypes
import numpy as np
from jax import lax
from jax.experimental import pallas as pl
from jax.experimental.pallas import tpu as pltpu
from jax.sharding import PartitionSpec as P

LAGS = 256
STEPS = 3
LANES = 128
GROUP = 16
MESH = pl.DeviceIdType.MESH


def dft_tables(length):
    bins = length // 2
    phase = np.mod(np.arange(length)[:, None] * np.arange(bins)[None, :], length)
    angle = 2.0 * np.pi * phase / length
    return np.cos(angle).astype(np.float32), (-np.sin(angle)).astype(np.float32)


def lag_tables(length):
    bins = length // 2
    phase = np.mod((np.arange(LAGS) - LAGS // 2)[:, None] * np.arange(bins)[None, :], length)
    angle = 2.0 * np.pi * phase / length
    both = np.stack([np.cos(angle), -np.sin(angle)], axis=1).astype(np.float32)
    return both.astype(ml_dtypes.bfloat16)


def regroup_table(segs):
    per = LANES // GROUP
    table = np.zeros((segs, per, GROUP, per, segs, GROUP), np.float32)
    for s in range(segs):
        for q in range(per):
            for f in range(GROUP):
                table[s, q, f, q, s, f] = 1.0
    size = segs * LANES
    return table.reshape(size, size).astype(ml_dtypes.bfloat16)


def row_table(channels, segs):
    table = np.zeros((segs, channels, channels, segs), np.float32)
    for s in range(segs):
        for c in range(channels):
            table[s, c, c, s] = 1.0
    size = segs * channels
    return table.reshape(size, size).astype(ml_dtypes.bfloat16)


def mm(a, b):
    return jnp.dot(a, b, preferred_element_type=jnp.float32)


def mm_t(a, b):
    return lax.dot_general(a, b, (((1,), (1,)), ((), ())), preferred_element_type=jnp.float32)


def kernel(
    blks, grps, dims, normalise,
    rec_ref, flag_ref, row_ref, hi_hbm, lo_hbm, perm_hbm, lag_hbm,
    out_ref, count_ref,
    hi_ref, lo_ref, perm_ref, lag_ref, load_sem, buf, diag, cross, inv, recv_sem, hop_sem, peer_sem, sib_sem,
):
    channels, segs, bins, half = dims
    width = half * 2 * segs
    chunks = half // GROUP
    pair = channels // 2
    loads = [
        pltpu.make_async_copy(source, target, load_sem.at[n])
        for n, (source, target) in enumerate(
            ((hi_hbm, hi_ref), (lo_hbm, lo_ref), (perm_hbm, perm_ref), (lag_hbm, lag_ref)))
    ]
    for load in loads:
        load.start()
    b = lax.axis_index("blk")
    g = lax.axis_index("grp")
    sib = g + 1 - 2 * lax.rem(g, 2)
    peers = [lax.rem(g + 2 * d, grps) for d in range(1, grps // 2)]

    barrier = pltpu.get_barrier_semaphore()
    for k in range(1, STEPS):
        pl.semaphore_signal(barrier, inc=1, device_id={"blk": lax.rem(b + blks - k, blks)}, device_id_type=MESH)
    for other in peers + [sib]:
        pl.semaphore_signal(barrier, inc=1, device_id={"grp": other}, device_id_type=MESH)

    rec = mm(row_ref[...], rec_ref[...]).astype(jnp.bfloat16)
    loads[0].wait()
    spec = mm(rec, hi_ref[...])
    loads[1].wait()
    spec = spec + mm(rec, lo_ref[...])
    real = spec[:, :bins]
    imag = spec[:, bins:]
    power = real * real + imag * imag
    level = jnp.sum(power, axis=1, keepdims=True) / bins
    scale = 1.0 / jnp.sqrt(power[:, :half] + level + 1e-06)
    flags = flag_ref[...]
    pieces = [(real[:, :half] * scale).astype(jnp.bfloat16), (imag[:, :half] * scale).astype(jnp.bfloat16)]
    rows = []
    for t in range(half // LANES):
        for piece in pieces:
            rows.append(jnp.concatenate([
                piece[s * channels:(s + 1) * channels, t * LANES:(t + 1) * LANES]
                * flags[:, s:s + 1].astype(jnp.bfloat16)
                for s in range(segs)
            ], axis=1))
    loads[2].wait()
    regrouped = mm(jnp.concatenate(rows, axis=0), perm_ref[...]).astype(jnp.bfloat16)
    per = LANES // GROUP
    for t in range(half // LANES):
        for i in range(2):
            part = regrouped[(t * 2 + i) * channels:(t * 2 + i + 1) * channels]
            for q in range(per):
                at = ((t * per + q) * 2 + i) * LANES
                buf[0, g, :, at:at + LANES] = part[:, q * LANES:(q + 1) * LANES]
    buf[0, g, :, width:width + LANES] = flags.astype(jnp.bfloat16)

    pl.semaphore_wait(barrier, STEPS - 1 + len(peers) + 1)

    sent = []

    cut = width // 2
    spans = [(0, cut), (cut, width + LANES - cut)]
    steps = [(k, h) for k in range(STEPS) for h in range(2)]

    def piece(k, h, slot):
        return buf.at[k, slot, :, pl.ds(*spans[h])]

    def send(source, target, send_sem, landed, where):
        copy = pltpu.make_async_remote_copy(
            src_ref=source, dst_ref=target, send_sem=send_sem, recv_sem=landed,
            device_id=where, device_id_type=MESH,
        )
        copy.start()
        sent.append(copy)

    def arrived(k, h, slot):
        ref = piece(k, h, slot)
        pltpu.make_async_copy(ref, ref, recv_sem.at[k, h, slot]).wait()

    def hand(k, h, slot, n):
        ref = piece(k, h, slot)
        send(ref, ref, sib_sem.at[k, h, n], recv_sem.at[k, h, slot], {"grp": sib})

    def spread(k, h):
        ref = piece(k, h, g)
        for d, other in enumerate(peers):
            send(ref, ref, peer_sem.at[k, h, d], recv_sem.at[k, h, g], {"grp": other})
        hand(k, h, g, 0)

    def hopped(k):
        for h in range(2):
            arrived(k, h, g)
            spread(k, h)

    def forward(k, h):
        for d in range(len(peers)):
            slot = lax.rem(g + grps - 2 * (d + 1), grps)
            arrived(k, h, slot)
            hand(k, h, slot, d + 1)

    def gather(k, h):
        for d in range(grps // 2):
            arrived(k, h, lax.rem(sib + 2 * d, grps))

    spread(0, 0)
    for k in range(1, STEPS):
        for h in range(2):
            send(piece(0, h, g), piece(k, h, g), hop_sem.at[k, h], recv_sem.at[k, h, g],
                 {"blk": lax.rem(b + k, blks)})
    spread(0, 1)

    size = 2 * segs * GROUP
    same = (lax.broadcasted_iota(jnp.int32, (channels * GROUP, size), 0) % GROUP
            == lax.broadcasted_iota(jnp.int32, (channels * GROUP, size), 1) % GROUP)

    def build(q, carry):
        at = pl.multiple_of(q * size, size)
        first = buf[0, g, :, pl.ds(at, size)].astype(jnp.float32)
        second = jnp.concatenate([first[:, LANES:], -first[:, :LANES]], axis=1)
        for i, value in enumerate((first, second)):
            wide = jnp.broadcast_to(value[:, None, :], (channels, GROUP, size)).reshape(channels * GROUP, size)
            diag[q, i * channels * GROUP:(i + 1) * channels * GROUP, :] = jnp.where(same, wide, 0.0).astype(jnp.bfloat16)
        return carry

    lax.fori_loop(0, chunks // 2, build, 0)
    hopped(1)
    forward(0, 0)
    lax.fori_loop(chunks // 2, chunks, build, 0)
    hopped(2)
    forward(0, 1)
    loads[3].wait()
    block = grps * channels
    unroll = 4

    def multiply(group, carry, k):
        for u in range(unroll):
            q = group * unroll + u
            at = pl.multiple_of(q * size, size)
            other = buf[k, :, :, pl.ds(at, size)].reshape(block, size)
            product = mm_t(diag[q], other).astype(jnp.bfloat16).reshape(2, 2, pair, GROUP, block)
            low = pl.multiple_of(q * GROUP, GROUP)
            for i in range(2):
                for p in range(2):
                    cross[:, i, pl.ds(low, GROUP), p * block:(p + 1) * block] = product[i, p]
        return carry

    def lag(c, carry, k):
        total = mm(lag_ref[...], cross[c].reshape(2 * half, 2 * block)).astype(jnp.bfloat16)
        if normalise:
            total = (total.astype(jnp.float32) * inv[pl.ds(c, 1), :]).astype(jnp.bfloat16)
        out_ref[k, c] = total[:, :block]
        out_ref[k, c + pair] = total[:, block:]
        return carry

    groups = chunks // 2 // unroll
    for n, (k, h) in enumerate(steps):
        gather(k, h)
        lax.fori_loop(h * groups, (h + 1) * groups, functools.partial(multiply, k=k), 0)
        if n + 2 < len(steps):
            forward(*steps[n + 2])
        if h == 1:
            tile = buf[k, :, :, width:width + LANES].reshape(block, LANES)
            count = mm_t(flags.astype(jnp.bfloat16), tile)
            count_ref[:, k * block:(k + 1) * block] = count
            factor = lax.rsqrt(bins * jnp.maximum(count, 1.0))
            inv[:, :block] = factor[:pair]
            inv[:, block:] = factor[pair:]
            lax.fori_loop(0, pair, functools.partial(lag, k=k), 0)

    for copy in sent:
        copy.wait_send()


def on_device(records, flags):
    channels, segs, length = records.shape
    bins = length // 2
    splits = lax.axis_size("sub")
    blks = lax.axis_size("blk")
    grps = lax.axis_size("grp")
    half = bins // splits
    block = grps * channels
    cos, sin = dft_tables(length)
    lags = lag_tables(length)
    both = np.stack([cos, sin], axis=1)
    high = both.astype(ml_dtypes.bfloat16)
    low = (both - high.astype(np.float32)).astype(ml_dtypes.bfloat16)
    high, low, lags = jnp.asarray(high), jnp.asarray(low), jnp.asarray(lags)
    if splits > 1:
        first = lax.axis_index("sub") * half
        high = jnp.roll(high, -first, axis=2)
        low = jnp.roll(low, -first, axis=2)
        lags = lax.dynamic_slice_in_dim(lags, first, half, 2)
    width = half * 2 * segs + LANES
    wide_flags = jnp.pad(flags.astype(jnp.float32), ((0, 0), (0, LANES - segs)))
    vmem = pl.BlockSpec(memory_space=pltpu.VMEM)
    out, count = pl.pallas_call(
        functools.partial(kernel, blks, grps, (channels, segs, bins, half), splits == 1),
        out_shape=(
            jax.ShapeDtypeStruct((STEPS, channels, LAGS, block), jnp.bfloat16),
            jax.ShapeDtypeStruct((channels, STEPS * block), jnp.float32),
        ),
        in_specs=[vmem] * 3 + [pl.BlockSpec(memory_space=pltpu.HBM)] * 4,
        out_specs=(vmem, vmem),
        scratch_shapes=[
            pltpu.VMEM((length, 2 * bins), jnp.bfloat16),
            pltpu.VMEM((length, 2 * bins), jnp.bfloat16),
            pltpu.VMEM((segs * LANES, segs * LANES), jnp.bfloat16),
            pltpu.VMEM((LAGS, 2 * half), jnp.bfloat16),
            pltpu.SemaphoreType.DMA((4,)),
            pltpu.VMEM((STEPS, grps, channels, width), jnp.bfloat16),
            pltpu.VMEM((half // GROUP, 2 * channels * GROUP, 2 * segs * GROUP), jnp.bfloat16),
            pltpu.VMEM((channels // 2, 2, half, 2 * block), jnp.bfloat16),
            pltpu.VMEM((channels // 2, 2 * block), jnp.float32),
            pltpu.SemaphoreType.DMA((STEPS, 2, grps)),
            pltpu.SemaphoreType.DMA((STEPS, 2)),
            pltpu.SemaphoreType.DMA((STEPS, 2, max(grps // 2 - 1, 1))),
            pltpu.SemaphoreType.DMA((STEPS, 2, grps // 2)),
        ],
        compiler_params=pltpu.CompilerParams(
            collective_id=0, has_side_effects=True, vmem_limit_bytes=62 * 1024 * 1024
        ),
    )(
        records.reshape(channels * segs, length),
        wide_flags,
        jnp.asarray(row_table(channels, segs)),
        high.reshape(length, 2 * bins),
        low.reshape(length, 2 * bins),
        jnp.asarray(regroup_table(segs)),
        lags.reshape(LAGS, 2 * half),
    )
    out = out.transpose(2, 1, 0, 3)
    if splits > 1:
        out = lax.psum_scatter(out, "sub", scatter_dimension=0, tiled=True).astype(jnp.float32)
        out = (out / jnp.sqrt(bins * jnp.maximum(count, 1.0)).reshape(1, channels, STEPS, block)).astype(jnp.bfloat16)
    return out


def solution(mesh):
    return jax.shard_map(
        on_device,
        mesh=mesh,
        in_specs=(P(("dom", "blk", "grp"), None, None), P(("dom", "blk", "grp"), None)),
        out_specs=P("sub", ("dom", "blk", "grp"), None, None),
        check_vma=False,
    )
```

```python
import functools

import jax
import jax.numpy as jnp
import ml_dtypes
import numpy as np
from jax import lax
from jax.experimental import pallas as pl
from jax.experimental.pallas import tpu as pltpu
from jax.sharding import PartitionSpec as P

LAGS = 256
STEPS = 3
LANES = 128
GROUP = 16
MESH = pl.DeviceIdType.MESH


def dft_tables(length):
    bins = length // 2
    phase = np.mod(np.arange(length)[:, None] * np.arange(bins)[None, :], length)
    angle = 2.0 * np.pi * phase / length
    return np.cos(angle).astype(np.float32), (-np.sin(angle)).astype(np.float32)


def lag_tables(length):
    bins = length // 2
    phase = np.mod((np.arange(LAGS) - LAGS // 2)[:, None] * np.arange(bins)[None, :], length)
    angle = 2.0 * np.pi * phase / length
    both = np.stack([np.cos(angle), -np.sin(angle)], axis=1).astype(np.float32)
    return both.astype(ml_dtypes.bfloat16)


def regroup_table(segs):
    per = LANES // GROUP
    table = np.zeros((segs, per, GROUP, per, segs, GROUP), np.float32)
    for s in range(segs):
        for q in range(per):
            for f in range(GROUP):
                table[s, q, f, q, s, f] = 1.0
    size = segs * LANES
    return table.reshape(size, size).astype(ml_dtypes.bfloat16)


def row_table(channels, segs):
    table = np.zeros((segs, channels, channels, segs), np.float32)
    for s in range(segs):
        for c in range(channels):
            table[s, c, c, s] = 1.0
    size = segs * channels
    return table.reshape(size, size).astype(ml_dtypes.bfloat16)


def mm(a, b):
    return jnp.dot(a, b, preferred_element_type=jnp.float32)


def mm_t(a, b):
    return lax.dot_general(a, b, (((1,), (1,)), ((), ())), preferred_element_type=jnp.float32)


def kernel(
    blks, grps, dims, normalise,
    rec_ref, flag_ref, row_ref, hi_hbm, lo_hbm, perm_hbm, lag_hbm,
    out_ref, count_ref,
    hi_ref, lo_ref, perm_ref, lag_ref, load_sem, buf, diag, cross, inv, stage, recv_sem, hop_sem, peer_sem, sib_sem,
):
    channels, segs, bins, half = dims
    width = half * 2 * segs
    chunks = half // GROUP
    pair = channels // 2
    loads = [
        pltpu.make_async_copy(source, target, load_sem.at[n])
        for n, (source, target) in enumerate(
            ((hi_hbm, hi_ref), (lo_hbm, lo_ref), (perm_hbm, perm_ref), (lag_hbm, lag_ref)))
    ]
    for load in loads:
        load.start()
    b = lax.axis_index("blk")
    g = lax.axis_index("grp")
    sib = g + 1 - 2 * lax.rem(g, 2)
    peers = [lax.rem(g + 2 * d, grps) for d in range(1, grps // 2)]

    barrier = pltpu.get_barrier_semaphore()
    for k in range(1, STEPS):
        pl.semaphore_signal(barrier, inc=1, device_id={"blk": lax.rem(b + blks - k, blks)}, device_id_type=MESH)
    for other in peers + [sib]:
        pl.semaphore_signal(barrier, inc=1, device_id={"grp": other}, device_id_type=MESH)

    rec = mm(row_ref[...], rec_ref[...]).astype(jnp.bfloat16)
    loads[0].wait()
    spec = mm(rec, hi_ref[...])
    loads[1].wait()
    spec = spec + mm(rec, lo_ref[...])
    real = spec[:, :bins]
    imag = spec[:, bins:]
    power = real * real + imag * imag
    level = jnp.sum(power, axis=1, keepdims=True) / bins
    scale = 1.0 / jnp.sqrt(power[:, :half] + level + 1e-06)
    flags = flag_ref[...]
    pieces = [(real[:, :half] * scale).astype(jnp.bfloat16), (imag[:, :half] * scale).astype(jnp.bfloat16)]
    rows = []
    for t in range(half // LANES):
        for piece in pieces:
            rows.append(jnp.concatenate([
                piece[s * channels:(s + 1) * channels, t * LANES:(t + 1) * LANES]
                * flags[:, s:s + 1].astype(jnp.bfloat16)
                for s in range(segs)
            ], axis=1))
    loads[2].wait()
    regrouped = mm(jnp.concatenate(rows, axis=0), perm_ref[...]).astype(jnp.bfloat16)
    per = LANES // GROUP
    for t in range(half // LANES):
        for i in range(2):
            part = regrouped[(t * 2 + i) * channels:(t * 2 + i + 1) * channels]
            for q in range(per):
                at = ((t * per + q) * 2 + i) * LANES
                buf[0, g, :, at:at + LANES] = part[:, q * LANES:(q + 1) * LANES]
    buf[0, g, :, width:width + LANES] = flags.astype(jnp.bfloat16)

    pl.semaphore_wait(barrier, STEPS - 1 + len(peers) + 1)

    sent = []

    cut = width // 2
    spans = [(0, cut), (cut, width + LANES - cut)]
    steps = [(k, h) for k in range(STEPS) for h in range(2)]

    def piece(k, h, slot):
        return buf.at[k, slot, :, pl.ds(*spans[h])]

    def send(source, target, send_sem, landed, where):
        copy = pltpu.make_async_remote_copy(
            src_ref=source, dst_ref=target, send_sem=send_sem, recv_sem=landed,
            device_id=where, device_id_type=MESH,
        )
        copy.start()
        sent.append(copy)

    def arrived(k, h, slot):
        ref = piece(k, h, slot)
        pltpu.make_async_copy(ref, ref, recv_sem.at[k, h, slot]).wait()

    def hand(k, h, slot, n):
        ref = piece(k, h, slot)
        send(ref, ref, sib_sem.at[k, h, n], recv_sem.at[k, h, slot], {"grp": sib})

    def spread(k, h):
        ref = piece(k, h, g)
        for d, other in enumerate(peers):
            send(ref, ref, peer_sem.at[k, h, d], recv_sem.at[k, h, g], {"grp": other})
        hand(k, h, g, 0)

    def hopped(k):
        for h in range(2):
            arrived(k, h, g)
            spread(k, h)

    def forward(k, h):
        for d in range(len(peers)):
            slot = lax.rem(g + grps - 2 * (d + 1), grps)
            arrived(k, h, slot)
            hand(k, h, slot, d + 1)

    def gather(k, h):
        for d in range(grps // 2):
            arrived(k, h, lax.rem(sib + 2 * d, grps))

    spread(0, 0)
    for k in range(1, STEPS):
        for h in range(2):
            send(piece(0, h, g), piece(k, h, g), hop_sem.at[k, h], recv_sem.at[k, h, g],
                 {"blk": lax.rem(b + k, blks)})
    spread(0, 1)

    size = 2 * segs * GROUP
    same = (lax.broadcasted_iota(jnp.int32, (channels * GROUP, size), 0) % GROUP
            == lax.broadcasted_iota(jnp.int32, (channels * GROUP, size), 1) % GROUP)

    def build(q, carry):
        at = pl.multiple_of(q * size, size)
        first = buf[0, g, :, pl.ds(at, size)].astype(jnp.float32)
        second = jnp.concatenate([first[:, LANES:], -first[:, :LANES]], axis=1)
        for i, value in enumerate((first, second)):
            wide = jnp.broadcast_to(value[:, None, :], (channels, GROUP, size)).reshape(channels * GROUP, size)
            diag[q, i * channels * GROUP:(i + 1) * channels * GROUP, :] = jnp.where(same, wide, 0.0).astype(jnp.bfloat16)
        return carry

    lax.fori_loop(0, chunks // 2, build, 0)
    hopped(1)
    forward(0, 0)
    lax.fori_loop(chunks // 2, chunks, build, 0)
    hopped(2)
    forward(0, 1)
    loads[3].wait()
    block = grps * channels
    unroll = 4

    def multiply(group, carry, k):
        for u in range(unroll):
            q = group * unroll + u
            at = pl.multiple_of(q * size, size)
            other = buf[k, :, :, pl.ds(at, size)].reshape(block, size)
            product = mm_t(diag[q], other).astype(jnp.bfloat16).reshape(2, 2, pair, GROUP, block)
            low = pl.multiple_of(q * GROUP, GROUP)
            for i in range(2):
                for p in range(2):
                    cross[:, i, pl.ds(low, GROUP), p * block:(p + 1) * block] = product[i, p]
        return carry

    def lag(c, carry, k):
        total = mm(lag_ref[...], cross[c].reshape(2 * half, 2 * block)).astype(jnp.bfloat16)
        if normalise:
            total = (total.astype(jnp.float32) * inv[pl.ds(c, 1), :]).astype(jnp.bfloat16)
        total = total.astype(jnp.float32)
        stage[pl.ds(c, LAGS, stride=channels), :] = total[:, :block]
        stage[pl.ds(c + pair, LAGS, stride=channels), :] = total[:, block:]
        return carry

    def place(n, carry, k):
        low = pl.multiple_of(n * 16, 16)
        part = stage[pl.ds(pl.multiple_of(n * 16 * channels, 16), 16 * channels), :]
        out_ref[pl.ds(low, 16), k] = part.astype(jnp.bfloat16).reshape(16, channels, block)
        return carry

    groups = chunks // 2 // unroll
    for n, (k, h) in enumerate(steps):
        gather(k, h)
        lax.fori_loop(h * groups, (h + 1) * groups, functools.partial(multiply, k=k), 0)
        if n + 2 < len(steps):
            forward(*steps[n + 2])
        if h == 1:
            tile = buf[k, :, :, width:width + LANES].reshape(block, LANES)
            count = mm_t(flags.astype(jnp.bfloat16), tile)
            count_ref[:, k * block:(k + 1) * block] = count
            factor = lax.rsqrt(bins * jnp.maximum(count, 1.0))
            inv[:, :block] = factor[:pair]
            inv[:, block:] = factor[pair:]
            lax.fori_loop(0, pair, functools.partial(lag, k=k), 0)
            lax.fori_loop(0, LAGS // 16, functools.partial(place, k=k), 0)

    for copy in sent:
        copy.wait_send()


def on_device(records, flags):
    channels, segs, length = records.shape
    bins = length // 2
    splits = lax.axis_size("sub")
    blks = lax.axis_size("blk")
    grps = lax.axis_size("grp")
    half = bins // splits
    block = grps * channels
    cos, sin = dft_tables(length)
    lags = lag_tables(length)
    both = np.stack([cos, sin], axis=1)
    high = both.astype(ml_dtypes.bfloat16)
    low = (both - high.astype(np.float32)).astype(ml_dtypes.bfloat16)
    high, low, lags = jnp.asarray(high), jnp.asarray(low), jnp.asarray(lags)
    if splits > 1:
        first = lax.axis_index("sub") * half
        high = jnp.roll(high, -first, axis=2)
        low = jnp.roll(low, -first, axis=2)
        lags = lax.dynamic_slice_in_dim(lags, first, half, 2)
    width = half * 2 * segs + LANES
    wide_flags = jnp.pad(flags.astype(jnp.float32), ((0, 0), (0, LANES - segs)))
    vmem = pl.BlockSpec(memory_space=pltpu.VMEM)
    out, count = pl.pallas_call(
        functools.partial(kernel, blks, grps, (channels, segs, bins, half), splits == 1),
        out_shape=(
            jax.ShapeDtypeStruct((LAGS, STEPS, channels, block), jnp.bfloat16),
            jax.ShapeDtypeStruct((channels, STEPS * block), jnp.float32),
        ),
        in_specs=[vmem] * 3 + [pl.BlockSpec(memory_space=pltpu.HBM)] * 4,
        out_specs=(vmem, vmem),
        scratch_shapes=[
            pltpu.VMEM((length, 2 * bins), jnp.bfloat16),
            pltpu.VMEM((length, 2 * bins), jnp.bfloat16),
            pltpu.VMEM((segs * LANES, segs * LANES), jnp.bfloat16),
            pltpu.VMEM((LAGS, 2 * half), jnp.bfloat16),
            pltpu.SemaphoreType.DMA((4,)),
            pltpu.VMEM((STEPS, grps, channels, width), jnp.bfloat16),
            pltpu.VMEM((half // GROUP, 2 * channels * GROUP, 2 * segs * GROUP), jnp.bfloat16),
            pltpu.VMEM((channels // 2, 2, half, 2 * block), jnp.bfloat16),
            pltpu.VMEM((channels // 2, 2 * block), jnp.float32),
            pltpu.VMEM(((LAGS + 1) * channels, block), jnp.float32),
            pltpu.SemaphoreType.DMA((STEPS, 2, grps)),
            pltpu.SemaphoreType.DMA((STEPS, 2)),
            pltpu.SemaphoreType.DMA((STEPS, 2, max(grps // 2 - 1, 1))),
            pltpu.SemaphoreType.DMA((STEPS, 2, grps // 2)),
        ],
        compiler_params=pltpu.CompilerParams(
            collective_id=0, has_side_effects=True, vmem_limit_bytes=62 * 1024 * 1024
        ),
    )(
        records.reshape(channels * segs, length),
        wide_flags,
        jnp.asarray(row_table(channels, segs)),
        high.reshape(length, 2 * bins),
        low.reshape(length, 2 * bins),
        jnp.asarray(regroup_table(segs)),
        lags.reshape(LAGS, 2 * half),
    )
    out = out.transpose(0, 2, 1, 3)
    if splits > 1:
        out = lax.psum_scatter(out, "sub", scatter_dimension=0, tiled=True).astype(jnp.float32)
        out = (out / jnp.sqrt(bins * jnp.maximum(count, 1.0)).reshape(1, channels, STEPS, block)).astype(jnp.bfloat16)
    return out


def solution(mesh):
    return jax.shard_map(
        on_device,
        mesh=mesh,
        in_specs=(P(("dom", "blk", "grp"), None, None), P(("dom", "blk", "grp"), None)),
        out_specs=P("sub", ("dom", "blk", "grp"), None, None),
        check_vma=False,
    )
```

```python
import functools

import jax
import jax.numpy as jnp
import ml_dtypes
import numpy as np
from jax import lax
from jax.experimental import pallas as pl
from jax.experimental.pallas import tpu as pltpu
from jax.sharding import PartitionSpec as P

LAGS = 256
STEPS = 3
LANES = 128
GROUP = 16
MESH = pl.DeviceIdType.MESH


def dft_tables(length):
    bins = length // 2
    phase = np.mod(np.arange(length)[:, None] * np.arange(bins)[None, :], length)
    angle = 2.0 * np.pi * phase / length
    return np.cos(angle).astype(np.float32), (-np.sin(angle)).astype(np.float32)


def lag_tables(length):
    bins = length // 2
    phase = np.mod((np.arange(LAGS) - LAGS // 2)[:, None] * np.arange(bins)[None, :], length)
    angle = 2.0 * np.pi * phase / length
    both = np.stack([np.cos(angle), -np.sin(angle)], axis=1).astype(np.float32)
    return both.astype(ml_dtypes.bfloat16)


def regroup_table(segs):
    per = LANES // GROUP
    table = np.zeros((segs, per, GROUP, per, segs, GROUP), np.float32)
    for s in range(segs):
        for q in range(per):
            for f in range(GROUP):
                table[s, q, f, q, s, f] = 1.0
    size = segs * LANES
    return table.reshape(size, size).astype(ml_dtypes.bfloat16)


def row_table(channels, segs):
    table = np.zeros((segs, channels, channels, segs), np.float32)
    for s in range(segs):
        for c in range(channels):
            table[s, c, c, s] = 1.0
    size = segs * channels
    return table.reshape(size, size).astype(ml_dtypes.bfloat16)


def mm(a, b):
    return jnp.dot(a, b, preferred_element_type=jnp.float32)


def mm_t(a, b):
    return lax.dot_general(a, b, (((1,), (1,)), ((), ())), preferred_element_type=jnp.float32)


def kernel(
    blks, grps, dims, normalise,
    rec_ref, flag_ref, row_ref, hi_hbm, lo_hbm, perm_hbm, lag_hbm,
    out_ref, count_ref,
    hi_ref, lo_ref, perm_ref, lag_ref, load_sem, buf, diag, cross, inv, stage, recv_sem, hop_sem, peer_sem, sib_sem,
):
    channels, segs, bins, half = dims
    width = half * 2 * segs
    chunks = half // GROUP
    pair = channels // 2
    loads = [
        pltpu.make_async_copy(source, target, load_sem.at[n])
        for n, (source, target) in enumerate(
            ((hi_hbm, hi_ref), (lo_hbm, lo_ref), (perm_hbm, perm_ref), (lag_hbm, lag_ref)))
    ]
    for load in loads:
        load.start()
    b = lax.axis_index("blk")
    g = lax.axis_index("grp")
    sib = g + 1 - 2 * lax.rem(g, 2)
    peers = [lax.rem(g + 2 * d, grps) for d in range(1, grps // 2)]

    barrier = pltpu.get_barrier_semaphore()
    for k in range(1, STEPS):
        pl.semaphore_signal(barrier, inc=1, device_id={"blk": lax.rem(b + blks - k, blks)}, device_id_type=MESH)
    for other in peers + [sib]:
        pl.semaphore_signal(barrier, inc=1, device_id={"grp": other}, device_id_type=MESH)

    rec = mm(row_ref[...], rec_ref[...]).astype(jnp.bfloat16)
    loads[0].wait()
    spec = mm(rec, hi_ref[...])
    loads[1].wait()
    spec = spec + mm(rec, lo_ref[...])
    real = spec[:, :bins]
    imag = spec[:, bins:]
    power = real * real + imag * imag
    level = jnp.sum(power, axis=1, keepdims=True) / bins
    scale = 1.0 / jnp.sqrt(power[:, :half] + level + 1e-06)
    flags = flag_ref[...]
    pieces = [(real[:, :half] * scale).astype(jnp.bfloat16), (imag[:, :half] * scale).astype(jnp.bfloat16)]
    rows = []
    for t in range(half // LANES):
        for piece in pieces:
            rows.append(jnp.concatenate([
                piece[s * channels:(s + 1) * channels, t * LANES:(t + 1) * LANES]
                * flags[:, s:s + 1].astype(jnp.bfloat16)
                for s in range(segs)
            ], axis=1))
    loads[2].wait()
    regrouped = mm(jnp.concatenate(rows, axis=0), perm_ref[...]).astype(jnp.bfloat16)
    per = LANES // GROUP
    for t in range(half // LANES):
        for i in range(2):
            part = regrouped[(t * 2 + i) * channels:(t * 2 + i + 1) * channels]
            for q in range(per):
                at = ((t * per + q) * 2 + i) * LANES
                buf[0, g, :, at:at + LANES] = part[:, q * LANES:(q + 1) * LANES]
    buf[0, g, :, width:width + LANES] = flags.astype(jnp.bfloat16)

    pl.semaphore_wait(barrier, STEPS - 1 + len(peers) + 1)

    sent = []

    cut = width // 2
    spans = [(0, cut), (cut, width + LANES - cut)]
    steps = [(k, h) for k in range(STEPS) for h in range(2)]

    def piece(k, h, slot):
        return buf.at[k, slot, :, pl.ds(*spans[h])]

    def send(source, target, send_sem, landed, where):
        copy = pltpu.make_async_remote_copy(
            src_ref=source, dst_ref=target, send_sem=send_sem, recv_sem=landed,
            device_id=where, device_id_type=MESH,
        )
        copy.start()
        sent.append(copy)

    def arrived(k, h, slot):
        ref = piece(k, h, slot)
        pltpu.make_async_copy(ref, ref, recv_sem.at[k, h, slot]).wait()

    def hand(k, h, slot, n):
        ref = piece(k, h, slot)
        send(ref, ref, sib_sem.at[k, h, n], recv_sem.at[k, h, slot], {"grp": sib})

    def spread(k, h):
        ref = piece(k, h, g)
        for d, other in enumerate(peers):
            send(ref, ref, peer_sem.at[k, h, d], recv_sem.at[k, h, g], {"grp": other})
        hand(k, h, g, 0)

    def hopped(k):
        for h in range(2):
            arrived(k, h, g)
            spread(k, h)

    def forward(k, h):
        for d in range(len(peers)):
            slot = lax.rem(g + grps - 2 * (d + 1), grps)
            arrived(k, h, slot)
            hand(k, h, slot, d + 1)

    def gather(k, h):
        for d in range(grps // 2):
            arrived(k, h, lax.rem(sib + 2 * d, grps))

    spread(0, 0)
    for k in range(1, STEPS):
        for h in range(2):
            send(piece(0, h, g), piece(k, h, g), hop_sem.at[k, h], recv_sem.at[k, h, g],
                 {"blk": lax.rem(b + k, blks)})
    spread(0, 1)

    size = 2 * segs * GROUP
    same = (lax.broadcasted_iota(jnp.int32, (channels * GROUP, size), 0) % GROUP
            == lax.broadcasted_iota(jnp.int32, (channels * GROUP, size), 1) % GROUP)

    def build(q, carry):
        at = pl.multiple_of(q * size, size)
        first = buf[0, g, :, pl.ds(at, size)].astype(jnp.float32)
        second = jnp.concatenate([first[:, LANES:], -first[:, :LANES]], axis=1)
        for i, value in enumerate((first, second)):
            wide = jnp.broadcast_to(value[:, None, :], (channels, GROUP, size)).reshape(channels * GROUP, size)
            diag[q, i * channels * GROUP:(i + 1) * channels * GROUP, :] = jnp.where(same, wide, 0.0).astype(jnp.bfloat16)
        return carry

    lax.fori_loop(0, chunks // 2, build, 0)
    hopped(1)
    forward(0, 0)
    lax.fori_loop(chunks // 2, chunks, build, 0)
    hopped(2)
    forward(0, 1)
    loads[3].wait()
    block = grps * channels
    unroll = 4

    def multiply(group, carry, k):
        for u in range(unroll):
            q = group * unroll + u
            at = pl.multiple_of(q * size, size)
            other = buf[k, :, :, pl.ds(at, size)].reshape(block, size)
            product = mm_t(diag[q], other).astype(jnp.bfloat16).reshape(2, 2, pair, GROUP, block)
            low = pl.multiple_of(q * GROUP, GROUP)
            for i in range(2):
                for p in range(2):
                    cross[:, i, pl.ds(low, GROUP), p * block:(p + 1) * block] = product[i, p]
        return carry

    def lag(c, carry, k):
        total = mm(lag_ref[...], cross[c].reshape(2 * half, 2 * block)).astype(jnp.bfloat16)
        if normalise:
            total = (total.astype(jnp.float32) * inv[pl.ds(c, 1), :]).astype(jnp.bfloat16)
        total = total.astype(jnp.float32)
        stage[pl.ds(c, LAGS, stride=channels), :] = total[:, :block]
        stage[pl.ds(c + pair, LAGS, stride=channels), :] = total[:, block:]
        return carry

    def place(n, carry, k):
        low = pl.multiple_of(n * 16, 16)
        part = stage[pl.ds(pl.multiple_of(n * 16 * channels, 16), 16 * channels), :]
        out_ref[pl.ds(low, 16), k] = part.astype(jnp.bfloat16).reshape(16, channels, block)
        return carry

    groups = chunks // 2 // unroll
    for n, (k, h) in enumerate(steps):
        gather(k, h)
        lax.fori_loop(h * groups, (h + 1) * groups, functools.partial(multiply, k=k), 0)
        if h == 1:
            tile = buf[k, :, :, width:width + LANES].reshape(block, LANES)
            count = mm_t(flags.astype(jnp.bfloat16), tile)
            count_ref[:, k * block:(k + 1) * block] = count
            factor = lax.rsqrt(bins * jnp.maximum(count, 1.0))
            inv[:, :block] = factor[:pair]
            inv[:, block:] = factor[pair:]
            lax.fori_loop(0, pair, functools.partial(lag, k=k), 0)
            lax.fori_loop(0, LAGS // 16, functools.partial(place, k=k), 0)
        if 0 < n < len(steps) - 1:
            forward(*steps[n + 1])

    for copy in sent:
        copy.wait_send()


def on_device(records, flags):
    channels, segs, length = records.shape
    bins = length // 2
    splits = lax.axis_size("sub")
    blks = lax.axis_size("blk")
    grps = lax.axis_size("grp")
    half = bins // splits
    block = grps * channels
    cos, sin = dft_tables(length)
    lags = lag_tables(length)
    both = np.stack([cos, sin], axis=1)
    high = both.astype(ml_dtypes.bfloat16)
    low = (both - high.astype(np.float32)).astype(ml_dtypes.bfloat16)
    high, low, lags = jnp.asarray(high), jnp.asarray(low), jnp.asarray(lags)
    if splits > 1:
        first = lax.axis_index("sub") * half
        high = jnp.roll(high, -first, axis=2)
        low = jnp.roll(low, -first, axis=2)
        lags = lax.dynamic_slice_in_dim(lags, first, half, 2)
    width = half * 2 * segs + LANES
    wide_flags = jnp.pad(flags.astype(jnp.float32), ((0, 0), (0, LANES - segs)))
    vmem = pl.BlockSpec(memory_space=pltpu.VMEM)
    out, count = pl.pallas_call(
        functools.partial(kernel, blks, grps, (channels, segs, bins, half), splits == 1),
        out_shape=(
            jax.ShapeDtypeStruct((LAGS, STEPS, channels, block), jnp.bfloat16),
            jax.ShapeDtypeStruct((channels, STEPS * block), jnp.float32),
        ),
        in_specs=[vmem] * 3 + [pl.BlockSpec(memory_space=pltpu.HBM)] * 4,
        out_specs=(vmem, vmem),
        scratch_shapes=[
            pltpu.VMEM((length, 2 * bins), jnp.bfloat16),
            pltpu.VMEM((length, 2 * bins), jnp.bfloat16),
            pltpu.VMEM((segs * LANES, segs * LANES), jnp.bfloat16),
            pltpu.VMEM((LAGS, 2 * half), jnp.bfloat16),
            pltpu.SemaphoreType.DMA((4,)),
            pltpu.VMEM((STEPS, grps, channels, width), jnp.bfloat16),
            pltpu.VMEM((half // GROUP, 2 * channels * GROUP, 2 * segs * GROUP), jnp.bfloat16),
            pltpu.VMEM((channels // 2, 2, half, 2 * block), jnp.bfloat16),
            pltpu.VMEM((channels // 2, 2 * block), jnp.float32),
            pltpu.VMEM(((LAGS + 1) * channels, block), jnp.float32),
            pltpu.SemaphoreType.DMA((STEPS, 2, grps)),
            pltpu.SemaphoreType.DMA((STEPS, 2)),
            pltpu.SemaphoreType.DMA((STEPS, 2, max(grps // 2 - 1, 1))),
            pltpu.SemaphoreType.DMA((STEPS, 2, grps // 2)),
        ],
        compiler_params=pltpu.CompilerParams(
            collective_id=0, has_side_effects=True, vmem_limit_bytes=62 * 1024 * 1024
        ),
    )(
        records.reshape(channels * segs, length),
        wide_flags,
        jnp.asarray(row_table(channels, segs)),
        high.reshape(length, 2 * bins),
        low.reshape(length, 2 * bins),
        jnp.asarray(regroup_table(segs)),
        lags.reshape(LAGS, 2 * half),
    )
    out = out.transpose(0, 2, 1, 3)
    if splits > 1:
        out = lax.psum_scatter(out, "sub", scatter_dimension=0, tiled=True).astype(jnp.float32)
        out = (out / jnp.sqrt(bins * jnp.maximum(count, 1.0)).reshape(1, channels, STEPS, block)).astype(jnp.bfloat16)
    return out


def solution(mesh):
    return jax.shard_map(
        on_device,
        mesh=mesh,
        in_specs=(P(("dom", "blk", "grp"), None, None), P(("dom", "blk", "grp"), None)),
        out_specs=P("sub", ("dom", "blk", "grp"), None, None),
        check_vma=False,
    )
```

```python
import functools

import jax
import jax.numpy as jnp
import ml_dtypes
import numpy as np
from jax import lax
from jax.experimental import pallas as pl
from jax.experimental.pallas import tpu as pltpu
from jax.sharding import PartitionSpec as P

LAGS = 256
STEPS = 3
LANES = 128
GROUP = 16
MESH = pl.DeviceIdType.MESH


def dft_tables(length):
    bins = length // 2
    phase = np.mod(np.arange(length)[:, None] * np.arange(bins)[None, :], length)
    angle = 2.0 * np.pi * phase / length
    return np.cos(angle).astype(np.float32), (-np.sin(angle)).astype(np.float32)


def lag_tables(length):
    bins = length // 2
    phase = np.mod((np.arange(LAGS) - LAGS // 2)[:, None] * np.arange(bins)[None, :], length)
    angle = 2.0 * np.pi * phase / length
    both = np.stack([np.cos(angle), -np.sin(angle)], axis=1).astype(np.float32)
    return both.astype(ml_dtypes.bfloat16)


def regroup_table(segs):
    per = LANES // GROUP
    table = np.zeros((segs, per, GROUP, per, segs, GROUP), np.float32)
    for s in range(segs):
        for q in range(per):
            for f in range(GROUP):
                table[s, q, f, q, s, f] = 1.0
    size = segs * LANES
    return table.reshape(size, size).astype(ml_dtypes.bfloat16)


def row_table(channels, segs):
    table = np.zeros((segs, channels, channels, segs), np.float32)
    for s in range(segs):
        for c in range(channels):
            table[s, c, c, s] = 1.0
    size = segs * channels
    return table.reshape(size, size).astype(ml_dtypes.bfloat16)


def mm(a, b):
    return jnp.dot(a, b, preferred_element_type=jnp.float32)


def mm_t(a, b):
    return lax.dot_general(a, b, (((1,), (1,)), ((), ())), preferred_element_type=jnp.float32)


def kernel(
    blks, grps, dims, normalise,
    rec_ref, flag_ref, row_ref, hi_hbm, lo_hbm, perm_hbm, lag_hbm,
    out_ref, count_ref,
    hi_ref, lo_ref, perm_ref, lag_ref, load_sem, buf, diag, cross, inv, wide, stage, recv_sem, hop_sem, peer_sem, sib_sem,
):
    channels, segs, bins, half = dims
    width = half * 2 * segs
    chunks = half // GROUP
    pair = channels // 2
    loads = [
        pltpu.make_async_copy(source, target, load_sem.at[n])
        for n, (source, target) in enumerate(
            ((hi_hbm, hi_ref), (lo_hbm, lo_ref), (perm_hbm, perm_ref), (lag_hbm, lag_ref)))
    ]
    for load in loads:
        load.start()
    b = lax.axis_index("blk")
    g = lax.axis_index("grp")
    sib = g + 1 - 2 * lax.rem(g, 2)
    peers = [lax.rem(g + 2 * d, grps) for d in range(1, grps // 2)]

    barrier = pltpu.get_barrier_semaphore()
    for k in range(1, STEPS):
        pl.semaphore_signal(barrier, inc=1, device_id={"blk": lax.rem(b + blks - k, blks)}, device_id_type=MESH)
    for other in peers + [sib]:
        pl.semaphore_signal(barrier, inc=1, device_id={"grp": other}, device_id_type=MESH)

    rec = mm(row_ref[...], rec_ref[...]).astype(jnp.bfloat16)
    loads[0].wait()
    spec = mm(rec, hi_ref[...])
    loads[1].wait()
    spec = spec + mm(rec, lo_ref[...])
    real = spec[:, :bins]
    imag = spec[:, bins:]
    power = real * real + imag * imag
    level = jnp.sum(power, axis=1, keepdims=True) / bins
    scale = 1.0 / jnp.sqrt(power[:, :half] + level + 1e-06)
    wide[...] = jnp.zeros_like(wide)
    wide[:, :segs] = flag_ref[...].astype(jnp.float32)
    flags = wide[...]
    pieces = [(real[:, :half] * scale).astype(jnp.bfloat16), (imag[:, :half] * scale).astype(jnp.bfloat16)]
    rows = []
    for t in range(half // LANES):
        for piece in pieces:
            rows.append(jnp.concatenate([
                piece[s * channels:(s + 1) * channels, t * LANES:(t + 1) * LANES]
                * flags[:, s:s + 1].astype(jnp.bfloat16)
                for s in range(segs)
            ], axis=1))
    loads[2].wait()
    regrouped = mm(jnp.concatenate(rows, axis=0), perm_ref[...]).astype(jnp.bfloat16)
    per = LANES // GROUP
    for t in range(half // LANES):
        for i in range(2):
            part = regrouped[(t * 2 + i) * channels:(t * 2 + i + 1) * channels]
            for q in range(per):
                at = ((t * per + q) * 2 + i) * LANES
                buf[0, g, :, at:at + LANES] = part[:, q * LANES:(q + 1) * LANES]
    buf[0, g, :, width:width + LANES] = flags.astype(jnp.bfloat16)

    pl.semaphore_wait(barrier, STEPS - 1 + len(peers) + 1)

    sent = []

    cut = width // 2
    spans = [(0, cut), (cut, width + LANES - cut)]
    steps = [(k, h) for k in range(STEPS) for h in range(2)]

    def piece(k, h, slot):
        return buf.at[k, slot, :, pl.ds(*spans[h])]

    def send(source, target, send_sem, landed, where):
        copy = pltpu.make_async_remote_copy(
            src_ref=source, dst_ref=target, send_sem=send_sem, recv_sem=landed,
            device_id=where, device_id_type=MESH,
        )
        copy.start()
        sent.append(copy)

    def arrived(k, h, slot):
        ref = piece(k, h, slot)
        pltpu.make_async_copy(ref, ref, recv_sem.at[k, h, slot]).wait()

    def hand(k, h, slot, n):
        ref = piece(k, h, slot)
        send(ref, ref, sib_sem.at[k, h, n], recv_sem.at[k, h, slot], {"grp": sib})

    def spread(k, h):
        ref = piece(k, h, g)
        for d, other in enumerate(peers):
            send(ref, ref, peer_sem.at[k, h, d], recv_sem.at[k, h, g], {"grp": other})
        hand(k, h, g, 0)

    def hopped(k):
        for h in range(2):
            arrived(k, h, g)
            spread(k, h)

    def forward(k, h):
        for d in range(len(peers)):
            slot = lax.rem(g + grps - 2 * (d + 1), grps)
            arrived(k, h, slot)
            hand(k, h, slot, d + 1)

    def gather(k, h):
        for d in range(grps // 2):
            arrived(k, h, lax.rem(sib + 2 * d, grps))

    spread(0, 0)
    for k in range(1, STEPS):
        for h in range(2):
            send(piece(0, h, g), piece(k, h, g), hop_sem.at[k, h], recv_sem.at[k, h, g],
                 {"blk": lax.rem(b + k, blks)})
    spread(0, 1)

    size = 2 * segs * GROUP
    same = (lax.broadcasted_iota(jnp.int32, (channels * GROUP, size), 0) % GROUP
            == lax.broadcasted_iota(jnp.int32, (channels * GROUP, size), 1) % GROUP)

    def build(q, carry):
        at = pl.multiple_of(q * size, size)
        first = buf[0, g, :, pl.ds(at, size)].astype(jnp.float32)
        second = jnp.concatenate([first[:, LANES:], -first[:, :LANES]], axis=1)
        for i, value in enumerate((first, second)):
            wide = jnp.broadcast_to(value[:, None, :], (channels, GROUP, size)).reshape(channels * GROUP, size)
            diag[q, i * channels * GROUP:(i + 1) * channels * GROUP, :] = jnp.where(same, wide, 0.0).astype(jnp.bfloat16)
        return carry

    lax.fori_loop(0, chunks // 2, build, 0)
    hopped(1)
    forward(0, 0)
    lax.fori_loop(chunks // 2, chunks, build, 0)
    hopped(2)
    forward(0, 1)
    loads[3].wait()
    block = grps * channels
    unroll = 4

    def multiply(group, carry, k):
        for u in range(unroll):
            q = group * unroll + u
            at = pl.multiple_of(q * size, size)
            other = buf[k, :, :, pl.ds(at, size)].reshape(block, size)
            product = mm_t(diag[q], other).astype(jnp.bfloat16).reshape(2, 2, pair, GROUP, block)
            low = pl.multiple_of(q * GROUP, GROUP)
            for i in range(2):
                for p in range(2):
                    cross[:, i, pl.ds(low, GROUP), p * block:(p + 1) * block] = product[i, p]
        return carry

    def lag(c, carry, k):
        total = mm(lag_ref[...], cross[c].reshape(2 * half, 2 * block)).astype(jnp.bfloat16)
        if normalise:
            total = (total.astype(jnp.float32) * inv[pl.ds(c, 1), :]).astype(jnp.bfloat16)
        total = total.astype(jnp.float32)
        stage[pl.ds(c, LAGS, stride=channels), :] = total[:, :block]
        stage[pl.ds(c + pair, LAGS, stride=channels), :] = total[:, block:]
        return carry

    def place(n, carry, k):
        low = pl.multiple_of(n * 16, 16)
        part = stage[pl.ds(pl.multiple_of(n * 16 * channels, 16), 16 * channels), :]
        out_ref[pl.ds(low, 16), k] = part.astype(jnp.bfloat16).reshape(16, channels, block)
        return carry

    groups = chunks // 2 // unroll
    for n, (k, h) in enumerate(steps):
        gather(k, h)
        lax.fori_loop(h * groups, (h + 1) * groups, functools.partial(multiply, k=k), 0)
        if n + 2 < len(steps):
            forward(*steps[n + 2])
        if h == 1:
            tile = buf[k, :, :, width:width + LANES].reshape(block, LANES)
            count = mm_t(flags.astype(jnp.bfloat16), tile)
            count_ref[:, k * block:(k + 1) * block] = count
            factor = lax.rsqrt(bins * jnp.maximum(count, 1.0))
            inv[:, :block] = factor[:pair]
            inv[:, block:] = factor[pair:]
            lax.fori_loop(0, pair, functools.partial(lag, k=k), 0)
            lax.fori_loop(0, LAGS // 16, functools.partial(place, k=k), 0)

    for copy in sent:
        copy.wait_send()


def on_device(records, flags):
    channels, segs, length = records.shape
    bins = length // 2
    splits = lax.axis_size("sub")
    blks = lax.axis_size("blk")
    grps = lax.axis_size("grp")
    half = bins // splits
    block = grps * channels
    cos, sin = dft_tables(length)
    lags = lag_tables(length)
    both = np.stack([cos, sin], axis=1)
    high = both.astype(ml_dtypes.bfloat16)
    low = (both - high.astype(np.float32)).astype(ml_dtypes.bfloat16)
    high, low, lags = jnp.asarray(high), jnp.asarray(low), jnp.asarray(lags)
    if splits > 1:
        first = lax.axis_index("sub") * half
        high = jnp.roll(high, -first, axis=2)
        low = jnp.roll(low, -first, axis=2)
        lags = lax.dynamic_slice_in_dim(lags, first, half, 2)
    width = half * 2 * segs + LANES
    vmem = pl.BlockSpec(memory_space=pltpu.VMEM)
    out, count = pl.pallas_call(
        functools.partial(kernel, blks, grps, (channels, segs, bins, half), splits == 1),
        out_shape=(
            jax.ShapeDtypeStruct((LAGS, STEPS, channels, block), jnp.bfloat16),
            jax.ShapeDtypeStruct((channels, STEPS * block), jnp.float32),
        ),
        in_specs=[vmem] * 3 + [pl.BlockSpec(memory_space=pltpu.HBM)] * 4,
        out_specs=(vmem, vmem),
        scratch_shapes=[
            pltpu.VMEM((length, 2 * bins), jnp.bfloat16),
            pltpu.VMEM((length, 2 * bins), jnp.bfloat16),
            pltpu.VMEM((segs * LANES, segs * LANES), jnp.bfloat16),
            pltpu.VMEM((LAGS, 2 * half), jnp.bfloat16),
            pltpu.SemaphoreType.DMA((4,)),
            pltpu.VMEM((STEPS, grps, channels, width), jnp.bfloat16),
            pltpu.VMEM((half // GROUP, 2 * channels * GROUP, 2 * segs * GROUP), jnp.bfloat16),
            pltpu.VMEM((channels // 2, 2, half, 2 * block), jnp.bfloat16),
            pltpu.VMEM((channels // 2, 2 * block), jnp.float32),
            pltpu.VMEM((channels, LANES), jnp.float32),
            pltpu.VMEM(((LAGS + 1) * channels, block), jnp.float32),
            pltpu.SemaphoreType.DMA((STEPS, 2, grps)),
            pltpu.SemaphoreType.DMA((STEPS, 2)),
            pltpu.SemaphoreType.DMA((STEPS, 2, max(grps // 2 - 1, 1))),
            pltpu.SemaphoreType.DMA((STEPS, 2, grps // 2)),
        ],
        compiler_params=pltpu.CompilerParams(
            collective_id=0, has_side_effects=True, vmem_limit_bytes=62 * 1024 * 1024
        ),
    )(
        records.reshape(channels * segs, length),
        flags,
        jnp.asarray(row_table(channels, segs)),
        high.reshape(length, 2 * bins),
        low.reshape(length, 2 * bins),
        jnp.asarray(regroup_table(segs)),
        lags.reshape(LAGS, 2 * half),
    )
    out = out.transpose(0, 2, 1, 3)
    if splits > 1:
        out = lax.psum_scatter(out, "sub", scatter_dimension=0, tiled=True).astype(jnp.float32)
        out = (out / jnp.sqrt(bins * jnp.maximum(count, 1.0)).reshape(1, channels, STEPS, block)).astype(jnp.bfloat16)
    return out


def solution(mesh):
    return jax.shard_map(
        on_device,
        mesh=mesh,
        in_specs=(P(("dom", "blk", "grp"), None, None), P(("dom", "blk", "grp"), None)),
        out_specs=P("sub", ("dom", "blk", "grp"), None, None),
        check_vma=False,
    )
```
